256 devices in a mesh: dp: 64 (over x, z_hi, y), mp: 4 (over z_lo, core).
Axes of the slice: x: 4, y: 4, z: 8 (z_hi: 4, z_lo: 2; z = z_hi * 2 + z_lo), core: 2. Of those that a mesh axis runs over, the one named last changes fastest.
Arguments:
- patch_feature_rows: bfloat16 [65536, 1152], P('dp'), may hold values from -250 to 250
- patch_picture_position: int32 [65536], P('dp'), may hold values from 0 to 63, as said below
- patch_row_tallies: int32 [64, 64], P('dp'), may hold values from 1 to 16, as said below
- pooling_seed_vector: bfloat16 [1152], replicated, may hold values from -6 to 6
- question_projection_factor: bfloat16 [1152, 1152], P(None, 'mp'), may hold values from -0.1875 to 0.1875
- lookup_projection_factor: bfloat16 [1152, 1152], P(None, 'mp'), may hold values from -0.1875 to 0.1875
- content_projection_factor: bfloat16 [1152, 1152], P(None, 'mp'), may hold values from -0.1875 to 0.1875
- result_projection_factor: bfloat16 [1152, 1152], P('mp'), may hold values from -0.1875 to 0.1875
- caption_tower_outputs: bfloat16 [4096, 1152], P(('dp', 'mp')), may hold values from -6 to 6
- partner_index_distance: int32 [4096], P('dp'), may hold values from 0 to 4095
- affinity_warmth_factor: float32 [1], replicated, may hold values from 4 to 16
- affinity_offset_term: float32 [1], replicated, may hold values from -3 to 0
Outputs:
- image_unit: bfloat16 [4096, 1152], P(('dp', 'mp'))
- picture_vector_derivative: float32 [4096, 1152], P(('dp', 'mp'))
- caption_vector_derivative: float32 [4096, 1152], P(('dp', 'mp'))
The draws below stay inside these ranges and needn't reach their ends.
Inputs may be any that keep to these rules, and one draw needn't show every extreme that they name: `patch_row_tallies`: entry [s, d] is the number of tile rows of index s of dp that go to owner d; one owner receives 16 rows from every index in every draw. `patch_picture_position`: every image of every owner receives at least one routed row.
All inputs are finite; a program needn't handle non-finite values.
Results may differ from the reference program's by a relative error of at most 0.014.
Values may be sent and summed in bfloat16 or wider, within the bound.
A program may use at most 64 MiB of HBM per device.

```python
import math
import jax
import jax.numpy as jnp
from jax import lax

HEADS = 16
HEAD_DIM = 72
D = 1152
RECV = 1024
IMG_DP = 64
IMAGES = 4096
TEXTS = 4096
CAP = 16
LEAST = 1
N_DP = 64


def route_counts(key):
    owners = RECV // CAP
    shared = jax.random.fold_in(key, 11)
    first_key, second_key, third_key = jax.random.split(shared, 3)
    owner_weight = jax.random.randint(first_key, (owners,), 1, 5)
    spread_range = (CAP - LEAST) * owner_weight // 4 + 1
    surplus = jax.random.randint(second_key, (owners, owners), 0, 1048576) % spread_range[None, :]
    fullest = jax.random.randint(third_key, (), 0, owners)
    columns = jnp.arange(owners)[None, :]
    return jnp.where(columns == fullest, CAP, LEAST + surplus).astype(jnp.int32)


def draw_patch_row_tallies(key, part):
    counts = route_counts(key)
    return counts


def draw_patch_picture_position(key, part):
    counts = route_counts(key)
    key = jax.random.fold_in(key, 5)
    owners = RECV // CAP
    row_ends = jnp.cumsum(counts, axis=1).astype(jnp.int32)
    starts = (row_ends - counts).astype(jnp.int32)
    positions = jnp.arange(RECV, dtype=jnp.int32)
    owner_of = jnp.sum((row_ends[:, :, None] <= positions[None, None, :]).astype(jnp.int32), axis=1)
    placed = owner_of < owners
    safe_owner = jnp.minimum(owner_of, owners - 1)
    within = positions[None, :] - jnp.take_along_axis(starts, safe_owner, axis=1)
    sources = jnp.arange(owners, dtype=jnp.int32)[:, None]
    forced = (sources * LEAST + within) % IMG_DP
    drawn = jax.random.randint(key, (owners, RECV), 0, IMG_DP)
    return jnp.where(placed & (within < LEAST), forced, drawn).reshape(-1).astype(jnp.int32)


def draw_patch_feature_rows(key, part):
    key = jax.random.fold_in(key, 7)
    base_key = jax.random.fold_in(key, 0)
    shape = (RECV * (RECV // CAP), D)
    base = jax.random.truncated_normal(base_key, -4.0, 4.0, shape, jnp.float32)
    return base.astype(jnp.bfloat16)


def plant(result, rng, least, top_value):
    longest = result.shape.index(max(result.shape))
    spots = []
    for shift in (0, 1):
        where = [jax.random.randint(jax.random.fold_in(rng, axis), (), 0, length) for axis, length in enumerate(result.shape)]
        where[longest] = (where[longest] + shift) % result.shape[longest]
        spots.append(tuple(where))
    return result.at[spots[0]].set(least).at[spots[1]].set(top_value)


def level_of(key, extent, shards, least, top_value):
    factor_of = 1.0
    for position, parts in shards:
        heights = jax.random.uniform(jax.random.fold_in(jax.random.fold_in(key, 6), position), (parts,), jnp.float32, least / len(shards), top_value / len(shards))
        factor_of = factor_of * jnp.repeat(jnp.exp(heights), extent[position] // parts).reshape((-1,) + (1,) * (len(extent) - 1 - position))
    return factor_of


def gaussian(rng, extent, scale, most, cuts=(), held_as=jnp.bfloat16):
    gain = level_of(rng, extent, cuts, -0.22, 0.18) if cuts else 1.0
    values = jax.random.normal(rng, extent, jnp.float32) * scale * gain
    return jnp.minimum(jnp.maximum(values, -most), most).astype(held_as)


def setup_inputs(seed: int = 0) -> dict:
    streams_of = jax.random.split(jax.random.key(seed), 13)
    return {
        "patch_feature_rows": draw_patch_feature_rows(jax.random.fold_in(streams_of[12], 71), 0),
        "patch_picture_position": draw_patch_picture_position(jax.random.fold_in(streams_of[12], 71), 0),
        "patch_row_tallies": draw_patch_row_tallies(jax.random.fold_in(streams_of[12], 71), 0),
        "pooling_seed_vector": gaussian(streams_of[3], (D,), 1.0, 6.0),
        "question_projection_factor": gaussian(streams_of[4], (D, D), D ** -0.5, 0.1875, ((1, 4),)),
        "lookup_projection_factor": gaussian(streams_of[5], (D, D), D ** -0.5, 0.1875, ((1, 4),)),
        "content_projection_factor": gaussian(streams_of[6], (D, D), D ** -0.5, 0.1875, ((1, 4),)),
        "result_projection_factor": gaussian(streams_of[7], (D, D), D ** -0.5, 0.1875, ((0, 4),)),
        "caption_tower_outputs": gaussian(streams_of[8], (TEXTS, D), 1.0, 6.0, ((0, 256),)),
        "partner_index_distance": plant(jax.random.randint(streams_of[9], (IMAGES,), 0, TEXTS), jax.random.fold_in(streams_of[9], 1), 0, TEXTS - 1).astype(jnp.int32),
        "affinity_warmth_factor": jnp.clip(jnp.exp(jax.random.uniform(streams_of[10], (1,), jnp.float32, math.log(4.0), math.log(16.0))), 4.0, 16.0),
        "affinity_offset_term": jnp.clip(jax.random.uniform(streams_of[11], (1,), jnp.float32, -3.0, 0.0), -3.0, 0.0),
    }


def unit_rows(matrix):
    widened = matrix.astype(jnp.float32)
    return (widened * lax.rsqrt(lax.optimization_barrier(jnp.sum(widened * widened, axis=-1, keepdims=True)) + 1e-06)).astype(jnp.bfloat16)

def reference(patch_feature_rows, patch_picture_position, patch_row_tallies, pooling_seed_vector, question_projection_factor, lookup_projection_factor, content_projection_factor, result_projection_factor, caption_tower_outputs, partner_index_distance, affinity_warmth_factor, affinity_offset_term):
    owners = N_DP
    factor = 1.0 / math.sqrt(HEAD_DIM)
    probe_query = jnp.dot(pooling_seed_vector[None, :], question_projection_factor, preferred_element_type=jnp.float32)[0]
    key_probe = jnp.einsum('dhc,hc->dh', lookup_projection_factor.astype(jnp.float32).reshape(D, HEADS, HEAD_DIM), probe_query.reshape(HEADS, HEAD_DIM), precision=lax.Precision.HIGHEST).astype(jnp.bfloat16)
    scores = jnp.dot(patch_feature_rows, key_probe, preferred_element_type=jnp.float32) * factor
    values = jnp.dot(patch_feature_rows, content_projection_factor, preferred_element_type=jnp.float32).astype(jnp.bfloat16)
    row_ends = jnp.cumsum(patch_row_tallies, axis=1).astype(jnp.int32)
    starts = (row_ends - patch_row_tallies).astype(jnp.int32)
    slot_ids = jnp.arange(CAP, dtype=jnp.int32)
    image_list = jnp.arange(IMG_DP, dtype=jnp.int32)
    source_base = jnp.arange(owners, dtype=jnp.int32) * RECV

    def pool_owner(columns):
        owner_counts, owner_starts = columns
        usable = slot_ids[None, :] < owner_counts[:, None]
        row_index = source_base[:, None] + owner_starts[:, None] + slot_ids[None, :]
        row_index = jnp.where(usable, row_index, 0).reshape(-1).astype(jnp.int32)
        image_ids = jnp.where(usable.reshape(-1), patch_picture_position[row_index], -1).astype(jnp.int32)
        score_rows = scores[row_index]
        value_rows = values[row_index]
        member = image_ids[None, :] == image_list[:, None]
        row_max = lax.optimization_barrier(jnp.max(jnp.where(member[:, :, None], score_rows[None, :, :], -jnp.inf), axis=1))
        row_top = row_max[jnp.maximum(image_ids, 0)]
        weights = jnp.where((image_ids >= 0)[:, None], jnp.exp(score_rows - row_top), 0.0)
        totals = jnp.dot(member.astype(jnp.float32), weights, precision=lax.Precision.HIGHEST)
        weighted = (weights[:, :, None] * value_rows.reshape(-1, HEADS, HEAD_DIM).astype(jnp.float32)).astype(jnp.bfloat16).reshape(-1, D)
        summed = jnp.dot(member.astype(jnp.bfloat16), weighted, preferred_element_type=jnp.float32)
        return (summed.reshape(IMG_DP, HEADS, HEAD_DIM) / totals[:, :, None]).reshape(IMG_DP, D).astype(jnp.bfloat16)
    pooled = lax.map(pool_owner, (patch_row_tallies.T, starts.T)).reshape(IMAGES, D)
    image_unit = unit_rows(jnp.dot(pooled, result_projection_factor, preferred_element_type=jnp.float32))
    caption_unit_length = unit_rows(caption_tower_outputs)
    exponent_warmth_factor = affinity_warmth_factor[0]
    affinity_offset_added = affinity_offset_term[0]
    text_ids = jnp.arange(TEXTS, dtype=jnp.int32)
    local_ids = jnp.arange(IMG_DP, dtype=jnp.int32)

    def pair_block(caption_vector_derivative, block):
        picture_feature_tile_group, offsets, first_image = block
        partner = (first_image + local_ids + offsets) % TEXTS
        couple_affinity_table = exponent_warmth_factor * jnp.dot(picture_feature_tile_group, caption_unit_length.T, preferred_element_type=jnp.float32) + affinity_offset_added
        labels = (partner[:, None] == text_ids[None, :]).astype(jnp.float32)
        logistic_derivative_values = (jax.nn.sigmoid(couple_affinity_table) - labels).astype(jnp.bfloat16)
        picture_vector_derivative = exponent_warmth_factor * jnp.dot(logistic_derivative_values, caption_unit_length, preferred_element_type=jnp.float32)
        caption_vector_derivative = caption_vector_derivative + exponent_warmth_factor * jnp.dot(logistic_derivative_values.T, picture_feature_tile_group, preferred_element_type=jnp.float32)
        return (caption_vector_derivative, picture_vector_derivative)
    blocks = (image_unit.reshape(N_DP, IMG_DP, D), partner_index_distance.reshape(N_DP, IMG_DP), jnp.arange(N_DP, dtype=jnp.int32) * IMG_DP)
    caption_vector_derivative, picture_vector_derivative = lax.scan(pair_block, jnp.zeros((TEXTS, D), jnp.float32), blocks)
    return (image_unit, picture_vector_derivative.reshape(IMAGES, D), caption_vector_derivative)
```

```python
import math

import jax
import jax.numpy as jnp
from jax import lax
from jax.experimental import pallas as pl
from jax.experimental.pallas import tpu as pltpu
from jax.sharding import PartitionSpec as P

MESH = pl.DeviceIdType.MESH
F32 = jnp.float32
BF16 = jnp.bfloat16

HEAD_DIM = 72
HEADS_HERE = 4
PART = 288
WIDE = 384
D = 1152
ROWS = 1024
CAP = 16
IMG = 64
TEXTS = 4096
LOW = -1e30


def iota(shape, dim):
    return lax.broadcasted_iota(jnp.int32, shape, dim)


def three_parts(value, which):
    first = value.astype(BF16).astype(F32)
    rest = value - first
    second = rest.astype(BF16).astype(F32)
    third = (rest - second).astype(BF16).astype(F32)
    return jnp.where(which == 0, first, jnp.where(which == 1, second, third))


def unit_rows(wide):
    return (wide * lax.rsqrt(jnp.sum(wide * wide, axis=-1, keepdims=True) + 1e-06)).astype(BF16)


def dot(a, b, dims=((1,), (0,))):
    return lax.dot_general(a, b, (dims, ((), ())), preferred_element_type=F32)


def kernel(
    x_hbm, pos_ref, tally_ref, seed_ref, wq_hbm, wk_hbm, wv_hbm, wo_hbm, cap_ref, dist_ref, warm_ref, offset_ref,
    unit_out, pict_out, text_out,
    x_v, wq, wk, wv, wext, v_all, send_a, recv_a, wo, send_z, recv_z, gath, txt, units,
    pict, core_s, core_r, line_s, line_r, cap_s, cap_r, cap_own,
    in_sem, x_sem, a_send, a_recv, t_send, t_recv, wo_send, wo_recv, z_send, z_recv,
    g_send, g_recv, f_send, core_send, core_recv, l_send, l_recv, c_send, c_recv,
):
    dp, mp = lax.axis_index("dp"), lax.axis_index("mp")
    x, zh, y = lax.div(dp, 16), lax.rem(lax.div(dp, 4), 4), lax.rem(dp, 4)
    zl, core = lax.div(mp, 2), lax.rem(mp, 2)
    z, xy = zh * 2 + zl, x * 4 + y
    mate = (dp, mp + 1 - 2 * core)

    def plane_place(q):
        return lax.rem(x + lax.div(q, 4), 4) * 4 + lax.rem(y + lax.rem(q, 4), 4)

    def plane_device(s):
        return (lax.div(s, 4) * 16 + zh * 4 + lax.rem(s, 4), mp)

    def line_device(zz):
        return (x * 16 + lax.div(zz, 2) * 4 + y, lax.rem(zz, 2) * 2 + core)

    def send(src, dst, send_sem, recv_sem, device):
        return pltpu.make_async_remote_copy(
            src_ref=src, dst_ref=dst, send_sem=send_sem, recv_sem=recv_sem, device_id=device, device_id_type=MESH
        )

    def each(low, high):
        def wrap(body):
            lax.fori_loop(low, high, lambda i, c: (body(i), c)[1], 0)

        return wrap

    loads = [
        pltpu.make_async_copy(wq_hbm, wq, in_sem.at[0]),
        pltpu.make_async_copy(wk_hbm, wk, in_sem.at[1]),
        pltpu.make_async_copy(wv_hbm, wv, in_sem.at[2]),
        pltpu.make_async_copy(wo_hbm, wo.at[mp], in_sem.at[3]),
    ]

    def x_load(i):
        rows = pl.ds(pl.multiple_of(i * 256, 256), 256)
        return pltpu.make_async_copy(x_hbm.at[rows], x_v.at[rows], x_sem.at[i])

    barrier = pltpu.get_barrier_semaphore()

    @each(1, 16)
    def _(q):
        pl.semaphore_signal(barrier, inc=1, device_id=plane_device(plane_place(q)), device_id_type=MESH)

    @each(1, 8)
    def _(o):
        pl.semaphore_signal(barrier, inc=1, device_id=line_device(lax.rem(z + o, 8)), device_id_type=MESH)

    pl.semaphore_signal(barrier, inc=1, device_id=mate, device_id_type=MESH)
    for load in loads[:3]:
        load.start()
    for i in range(4):
        x_load(i).start()
    loads[3].start()

    loads[0].wait()
    probe = dot(jnp.broadcast_to(seed_ref[...], (16, D)), wq[...])[0:1, :]
    col_head = lax.div(iota((128, PART), 1), HEAD_DIM)
    row_at = iota((128, PART), 0)
    at_head = (row_at >= 32) & (row_at < 44) & (lax.rem(row_at, 4) == col_head)
    probe_1 = probe.astype(BF16).astype(F32)
    probe_2 = (probe - probe_1).astype(BF16).astype(F32)
    probe_3 = probe - probe_1 - probe_2
    loads[1].wait()
    key_probe = jnp.zeros((D, 128), F32)
    for part in (probe_3, probe_2, probe_1):
        spread = jnp.where(at_head, jnp.broadcast_to(part, (128, PART)), 0.0).astype(BF16)
        key_probe += dot(wk[...], spread, ((1,), (1,)))
    wext[:, 256:384] = key_probe.astype(BF16)
    loads[2].wait()
    wext[:, 0:PART] = wv[...]

    counts = jnp.broadcast_to(tally_ref[...].astype(F32), (64, 64))
    up_to = iota((64, 64), 1) <= iota((64, 64), 0)
    same = iota((64, 64), 1) == iota((64, 64), 0)
    ends = jnp.sum(jnp.where(up_to, counts, 0.0), axis=1, keepdims=True)
    starts = ends - jnp.sum(jnp.where(same, counts, 0.0), axis=1, keepdims=True)
    row_number = iota((64, ROWS), 1).astype(F32)
    owner = jnp.sum(jnp.where(ends <= row_number, 1.0, 0.0), axis=0, keepdims=True).astype(jnp.int32)
    first = jnp.max(jnp.where(starts <= row_number, starts, 0.0), axis=0, keepdims=True)
    within = (row_number[0:1, :] - first).astype(jnp.int32)
    place = (owner >> 4) * 16 + (owner & 3) * 4 + ((owner >> 2) & 3)
    slot = place * CAP + within
    ids = jnp.transpose(pos_ref[...].astype(F32) + 1.0)

    lane = iota((256, 128), 1)
    which = lax.div(lane - 32, 4)

    @each(0, 4)
    def _(i):
        x_load(i).wait()
        rows = pl.ds(pl.multiple_of(i * 256, 256), 256)
        out = dot(x_v[rows, :], wext[...])
        v_all[rows, 0:256] = out[:, 0:256].astype(BF16)
        tail = out[:, 256:384]
        score = three_parts(tail * (1.0 / math.sqrt(HEAD_DIM)), which)
        lane8 = iota((128, 8), 1)
        number = jnp.concatenate(
            [jnp.sum(jnp.where(lane8 == 2 * i + b, ids, 0.0), axis=1, keepdims=True) for b in (0, 1)], axis=0
        )
        extra = jnp.where(lane == 44, number, jnp.where(lane == 45, 1.0, 0.0))
        tail = jnp.where(lane < 32, tail, jnp.where(lane < 44, score, extra))
        v_all[rows, 256:384] = tail.astype(BF16)

    pl.semaphore_wait(barrier, 23)

    loads[3].wait()
    up, down = lax.rem(z + 1, 8), lax.rem(z + 7, 8)
    far = (1 - zl) * 2 + core
    low_half, high_half = pl.ds(0, 144), pl.ds(144, 144)
    wo_low = send(wo.at[mp, low_half], wo.at[mp, low_half], wo_send.at[0], wo_recv.at[0], line_device(up))
    wo_high = send(wo.at[mp, high_half], wo.at[mp, high_half], wo_send.at[1], wo_recv.at[1], line_device(down))
    wo_mate = send(wo.at[mp], wo.at[mp], wo_send.at[2], wo_recv.at[2], mate)
    wo_fwd = send(wo.at[far], wo.at[far], wo_send.at[3], wo_recv.at[3], mate)
    wo_low.start()
    wo_high.start()
    wo_mate.start()

    def a_copy(q, recv=False):
        s = plane_place(q)
        at = s if recv else xy
        return send(send_a.at[s], recv_a.at[at], a_send.at[q], a_recv.at[at], plane_device(s))

    @each(0, 4)
    def _(i):
        ox = lax.rem(i + 1, 4)
        xx = lax.rem(x + ox, 4)
        pick = (iota((256, ROWS), 0) + xx * 256) == slot
        block = dot(jnp.where(pick, 1.0, 0.0).astype(BF16), v_all[...]).astype(BF16)
        send_a[pl.ds(xx * 4, 4)] = block.reshape(4, 64, WIDE)

        @pl.when(ox != 0)
        def _():
            a_copy(ox * 4).start()

        for oy in range(1, 4):
            a_copy(ox * 4 + oy).start()

    recv_a[xy] = send_a[xy]

    txt[xy] = unit_rows(cap_ref[...].astype(F32))

    def t_copy(q, recv=False):
        s = plane_place(q)
        at = s if recv else xy
        return send(txt.at[xy], txt.at[at], t_send.at[q], t_recv.at[at], plane_device(s))

    @each(1, 16)
    def _(q):
        t_copy(q).start()

    wo_low.wait_recv()
    wo_high.wait_recv()
    wo_fwd.start()

    @each(1, 16)
    def _(q):
        a_copy(q, True).wait_recv()

    pick_row, pick_lane = iota((16, 128), 0), iota((16, 128), 1)
    score_lane = (pick_lane >= 32) & (pick_lane < 44) & (lax.rem(pick_lane, 4) == pick_row) & (pick_row < 4)
    picker = jnp.where(score_lane | ((pick_row == 4) & (pick_lane == 44)), 1.0, 0.0).astype(BF16)
    lane64 = iota((64, 128), 1)
    wide_lane = iota((64, WIDE), 1)

    def by_head(lanes, items):
        return jnp.where(
            lanes == 0, items[0], jnp.where(lanes == 1, items[1], jnp.where(lanes == 2, items[2], items[3]))
        )

    def z_copy(o, recv=False):
        to = lax.rem(zh + o, 4)
        at = to if recv else zh
        return send(send_z.at[to], recv_z.at[at], z_send.at[o], z_recv.at[at], line_device(to * 2 + zl))

    @each(0, 4)
    def _(i):
        o = lax.rem(i + 1, 4)
        to = lax.rem(zh + o, 4)
        rows = recv_a[:, pl.ds(pl.multiple_of(to * CAP, CAP), CAP), :].reshape(256, WIDE)
        across = dot(picker, rows[:, 256:384], ((1,), (1,)))
        member = across[4:5, :] == (iota((64, 256), 0) + 1).astype(F32)
        tops, weights = [], []
        for h in range(HEADS_HERE):
            score = jnp.where(member, across[h : h + 1, :], LOW)
            top = jnp.max(score, axis=1, keepdims=True)
            tops.append(top)
            weights.append(jnp.where(member, jnp.exp(score - top), 0.0))
        sums = dot(jnp.concatenate(weights, axis=0).astype(BF16), rows)
        parts = [sums[64 * h : 64 * h + 64, :] for h in range(HEADS_HERE)]
        chosen = by_head(lax.div(wide_lane, HEAD_DIM), parts)
        head = lax.rem(lane64, 4)
        totals = [p[:, 301:302] for p in parts]
        stat = jnp.where(lane64 < 44, by_head(head, tops), by_head(head, totals))
        stat = three_parts(stat, lax.rem(lax.div(lane64 - 32, 4), 3))
        tail = jnp.where(lane64 < 32, chosen[:, 256:384], jnp.where((lane64 < 56), stat, 0.0))
        send_z[to, :, 0:256] = chosen[:, 0:256].astype(BF16)
        send_z[to, :, 256:384] = tail.astype(BF16)

        @pl.when(o != 0)
        def _():
            z_copy(o).start()

    recv_z[zh] = send_z[zh]
    partner = (
        jnp.sum(jnp.where(same, jnp.broadcast_to(dist_ref[...].astype(F32), (64, 64)), 0.0), axis=1, keepdims=True)
    ).astype(jnp.int32)
    partner = (partner + iota((64, 1), 0) + dp * IMG) & (TEXTS - 1)
    stat_row, stat_col = iota((128, WIDE), 0), lax.div(iota((128, WIDE), 1), HEAD_DIM)
    same_head = lax.rem(stat_row, 4) == stat_col
    to_top = jnp.where((stat_row >= 32) & (stat_row < 44) & same_head, 1.0, 0.0).astype(BF16)
    to_total = jnp.where((stat_row >= 44) & (stat_row < 56) & same_head, 1.0, 0.0).astype(BF16)

    @each(1, 4)
    def _(o):
        z_copy(o, True).wait_recv()

    stats = recv_z[:, :, 256:384].reshape(256, 128)
    top_all, total_all = dot(stats, to_top), dot(stats, to_total)
    tops = [top_all[64 * p : 64 * p + 64, :] for p in range(4)]
    top = jnp.maximum(jnp.maximum(tops[0], tops[1]), jnp.maximum(tops[2], tops[3]))
    total = jnp.zeros((64, WIDE), F32)
    summed = jnp.zeros((64, WIDE), F32)
    for p in range(4):
        scale = jnp.exp(tops[p] - top)
        total += scale * total_all[64 * p : 64 * p + 64, :]
        summed += scale * recv_z[p].astype(F32)
    pooled = summed / total
    high, low = (partner >> 6).astype(F32), (partner & 63).astype(F32)
    pooled = jnp.where(
        wide_lane < PART, pooled, jnp.where(wide_lane == PART, high, jnp.where(wide_lane == PART + 1, low, 0.0))
    )
    mine = mp * 4 + zh
    gath[mine] = pooled.astype(BF16)

    def line_step(i):
        odd, half = lax.rem(i, 2), lax.div(i, 2)
        return lax.rem(z + (1 - odd) * (1 + half) + odd * (7 - half), 8)

    def place_of(zz, cc):
        return (lax.rem(zz, 2) * 2 + cc) * 4 + lax.div(zz, 2)

    def g_copy(i, recv=False):
        zz = line_step(i)
        at = place_of(zz, core) if recv else mine
        return send(gath.at[mine], gath.at[at], g_send.at[i], g_recv.at[at], line_device(zz))

    def f_copy(i, recv=False):
        zz = line_step(i)
        src = place_of(zz, core)
        at = place_of(zz, 1 - core) if recv else src
        return send(gath.at[src], gath.at[at], f_send.at[i], g_recv.at[at], mate)

    def m_copy(recv=False):
        at = place_of(z, 1 - core) if recv else mine
        return send(gath.at[mine], gath.at[at], f_send.at[7], g_recv.at[at], mate)

    @each(0, 7)
    def _(i):
        g_copy(i).start()

    m_copy().start()

    @each(0, 7)
    def _(i):
        g_copy(i, True).wait_recv()
        f_copy(i).start()

    send(wo.at[mp], wo.at[mp + 1 - 2 * core], wo_send.at[2], wo_recv.at[2], mate).wait_recv()
    far_mate = (1 - zl) * 2 + 1 - core
    send(wo.at[far], wo.at[far_mate], wo_send.at[3], wo_recv.at[3], mate).wait_recv()
    m_copy(True).wait_recv()

    @each(0, 7)
    def _(i):
        f_copy(i, True).wait_recv()

    @each(0, 4)
    def _(i):
        total = jnp.zeros((64, D), F32)
        for m in range(4):
            total += dot(gath[m * 4 + i][:, 0:PART], wo[m])
        units[pl.ds(pl.multiple_of(i * 64, 64), 64), :] = unit_rows(total)

    unit_out[...] = units[pl.ds(pl.multiple_of((zh * 4 + mp) * 16, 16), 16), :]

    @each(1, 16)
    def _(q):
        t_copy(q, True).wait_recv()

    warmth, added = warm_ref[0], offset_ref[0]
    texts = txt[...].reshape(256, D)
    logits = warmth * dot(units[...], texts, ((1,), (1,))) + added
    ends_of = gath[0:4, :, 256:384].reshape(256, 128).astype(F32)
    lane256 = iota((256, 128), 1)
    partners = jnp.sum(
        jnp.where(lane256 == 32, ends_of * 64.0, jnp.where(lane256 == 33, ends_of, 0.0)), axis=1, keepdims=True
    )
    c = iota((1, 256), 1)
    text_id = ((((c >> 6) * 4 + zh) * 4 + ((c >> 4) & 3)) * 4 + mp) * 16 + (c & 15)
    slopes = jax.nn.sigmoid(logits) - jnp.where(partners == text_id.astype(F32), 1.0, 0.0)
    slopes = slopes.astype(BF16)

    pict[...] = dot(slopes, texts).reshape(16, 16, D)

    @each(0, 8)
    def _(i):
        core_s[i] = pict[2 * i + 1 - core].astype(BF16)

    core_copy = send(core_s, core_r, core_send, core_recv, mate)
    core_copy.start()

    cap = dot(slopes, units[...], ((0,), (0,))).reshape(16, 16, D)
    cap_own[...] = cap
    cap_s[...] = cap.astype(BF16)

    def c_copy(q, recv=False):
        s = plane_place(q)
        at = s if recv else xy
        return send(cap_s.at[s], cap_r.at[at], c_send.at[q], c_recv.at[at], plane_device(s))

    @each(1, 16)
    def _(q):
        c_copy(q).start()

    def l_copy(i, recv=False):
        zz = line_step(i)
        at = zz if recv else z
        return send(line_s.at[zz], line_r.at[at], l_send.at[i], l_recv.at[at], line_device(zz))

    core_copy.wait_recv()

    @each(0, 7)
    def _(i):
        zz = line_step(i)
        line_s[zz] = (pict[2 * zz + core] + core_r[zz].astype(F32)).astype(BF16)
        l_copy(i).start()

    pict_out[...] = pict[2 * z + core] + core_r[z].astype(F32)
    text_out[...] = cap_own[xy]

    @each(0, 7)
    def _(i):
        l_copy(i, True).wait_recv()
        pict_out[...] += line_r[line_step(i)].astype(F32)

    pict_out[...] = warmth * pict_out[...]

    @each(1, 16)
    def _(q):
        c_copy(q, True).wait_recv()
        text_out[...] += cap_r[plane_place(q)].astype(F32)

    text_out[...] = warmth * text_out[...]

    wo_low.wait_send()
    wo_high.wait_send()
    wo_mate.wait_send()
    wo_fwd.wait_send()
    core_copy.wait_send()
    m_copy().wait_send()

    @each(1, 4)
    def _(o):
        z_copy(o).wait_send()

    @each(0, 7)
    def _(i):
        g_copy(i).wait_send()
        f_copy(i).wait_send()
        l_copy(i).wait_send()

    @each(1, 16)
    def _(q):
        a_copy(q).wait_send()
        t_copy(q).wait_send()
        c_copy(q).wait_send()


def local(rows, position, tallies, seed, wq, wk, wv, wo, captions, distance, warmth, added):
    vmem, hbm = pl.BlockSpec(memory_space=pltpu.VMEM), pl.BlockSpec(memory_space=pl.ANY)
    smem = pl.BlockSpec(memory_space=pltpu.SMEM)
    dma = pltpu.SemaphoreType.DMA
    block = captions.shape
    return pl.pallas_call(
        kernel,
        out_shape=(
            jax.ShapeDtypeStruct(block, BF16),
            jax.ShapeDtypeStruct(block, F32),
            jax.ShapeDtypeStruct(block, F32),
        ),
        in_specs=[hbm, vmem, vmem, vmem, hbm, hbm, hbm, hbm, vmem, vmem, smem, smem],
        out_specs=(vmem, vmem, vmem),
        scratch_shapes=[
            pltpu.VMEM((ROWS, D), BF16),
            pltpu.VMEM((D, PART), BF16),
            pltpu.VMEM((D, PART), BF16),
            pltpu.VMEM((D, PART), BF16),
            pltpu.VMEM((D, WIDE), BF16),
            pltpu.VMEM((ROWS, WIDE), BF16),
            pltpu.VMEM((16, 64, WIDE), BF16),
            pltpu.VMEM((16, 64, WIDE), BF16),
            pltpu.VMEM((4, PART, D), BF16),
            pltpu.VMEM((4, 64, WIDE), BF16),
            pltpu.VMEM((4, 64, WIDE), BF16),
            pltpu.VMEM((16, 64, WIDE), BF16),
            pltpu.VMEM((16, 16, D), BF16),
            pltpu.VMEM((256, D), BF16),
            pltpu.VMEM((16, 16, D), F32),
            pltpu.VMEM((8, 16, D), BF16),
            pltpu.VMEM((8, 16, D), BF16),
            pltpu.VMEM((8, 16, D), BF16),
            pltpu.VMEM((8, 16, D), BF16),
            pltpu.VMEM((16, 16, D), BF16),
            pltpu.VMEM((16, 16, D), BF16),
            pltpu.VMEM((16, 16, D), F32),
            dma((4,)), dma((4,)),
            dma((16,)), dma((16,)),
            dma((16,)), dma((16,)),
            dma((4,)), dma((4,)),
            dma((4,)), dma((4,)),
            dma((7,)), dma((16,)), dma((8,)),
            dma, dma,
            dma((7,)), dma((8,)),
            dma((16,)), dma((16,)),
        ],
        compiler_params=pltpu.CompilerParams(
            collective_id=0, has_side_effects=True, vmem_limit_bytes=48 * 1024 * 1024
        ),
    )(
        rows, position.reshape(8, 128), tallies, seed.reshape(1, D), wq, wk, wv, wo, captions,
        distance.reshape(1, IMG), warmth, added,
    )


def solution(mesh):
    placed = (
        P("dp", None),
        P("dp"),
        P("dp", None),
        P(),
        P(None, "mp"),
        P(None, "mp"),
        P(None, "mp"),
        P("mp", None),
        P(("dp", "mp"), None),
        P("dp"),
        P(),
        P(),
    )
    return jax.shard_map(
        local,
        mesh=mesh,
        in_specs=placed,
        out_specs=(P(("dp", "mp"), None), P(("dp", "mp"), None), P(("dp", "mp"), None)),
        check_vma=False,
    )
```
